256 devices in a mesh: rows: 32 (over z, y), cols: 8 (over x, core).
Axes of the slice: x: 4, y: 4, z: 8, core: 2. Of those that a mesh axis runs over, the one named last changes fastest.
Arguments:
- right_side: float32 [32, 131072], P(None, ('rows', 'cols')), may hold values from -6 to 6
- blocks: float32 [3072, 512, 512], P(('rows', 'cols')), as said below
- slot_row: int32 [3072], P(('rows', 'cols')), may hold values from 0 to 255, as said below
- slot_col: int32 [3072], P(('rows', 'cols')), may hold values from 0 to 255, as said below
Outputs:
- solution: float32 [32, 131072], P(None, ('rows', 'cols'))
- residual: float32 [32, 131072], P(None, ('rows', 'cols'))
The draws below stay inside these ranges and needn't reach their ends.
Inputs may be any that keep to these rules, and one draw needn't show every extreme that they name: `slot_row`: device d (rows index r = d // 8, cols index c = d % 8) holds slots d * 12 to d * 12 + 11. Its first slot holds the diagonal block (d, d). Every other slot holds either a distinct strictly upper block (i, j) with i in r * 8 to r * 8 + 7, j > i, j % 8 = c and j // 8 in r to 31, or is empty: then it repeats (d, d) and its block is zero. Live slots come first; some device has all 12 slots live. `slot_col`: the block column of each slot, as described for slot_row. Diagonal blocks are symmetric; the assembled matrix A is symmetric positive definite.
All inputs are finite; a program needn't handle non-finite values.
Results may differ from the reference program's by a relative error of at most 0.0003.
Values sent between devices are 32-bit elements; how exact they have to be, the bound alone decides.
No kernel may reach another device: no remote copies, remote signals or barrier semaphores. Data moves between devices by JAX's collectives and lax.ppermute only.
A program may use at most 128 MiB of HBM per device.

```python
import math
import jax
import jax.numpy as jnp
from jax import lax

BLOCK = 512
SIDES = 32
SLOTS = 12
ITERS = 4
NBLK = 256
ORDER = 131072
N_ROWS = 32
N_COLS = 8
DEVICES = 256


def pattern(key):
    first_key, second_key, third_key = jax.random.split(key, 3)
    device_ids = jnp.arange(DEVICES, dtype=jnp.int32)
    group_row = device_ids // N_COLS
    group_col = device_ids % N_COLS
    candidate = jnp.arange(DEVICES, dtype=jnp.int32)
    block_rows = group_row[:, None] * N_COLS + (candidate // N_ROWS)[None, :]
    target_rows = (candidate % N_ROWS)[None, :]
    block_cols = target_rows * N_COLS + group_col[:, None]
    reach = target_rows - group_row[:, None]
    allowed = (block_cols > block_rows) & (reach >= 0)
    scores = jax.random.randint(first_key, (DEVICES, DEVICES), 0, 2 ** 20) * DEVICES + candidate[None, :]
    forced = (device_ids[:, None] == 0) & ((candidate[None, :] == N_ROWS // 2) | (candidate[None, :] == N_ROWS - 1))
    scores = jnp.where(forced, 2 ** 29 + candidate[None, :], scores)
    scores = jnp.where(allowed, scores, -1 - candidate[None, :])
    chosen = lax.top_k(scores, SLOTS - 1)[1]
    available = jnp.sum(allowed.astype(jnp.int32), axis=1)
    wanted = jax.random.randint(second_key, (DEVICES,), 1, SLOTS)
    fullest = jax.random.randint(third_key, (), 0, DEVICES // 2)
    wanted = jnp.where(device_ids == fullest, SLOTS - 1, wanted)
    wanted = jnp.where(device_ids == 0, jnp.maximum(wanted, 2), wanted)
    filled = jnp.minimum(wanted, available)
    live = jnp.arange(SLOTS - 1, dtype=jnp.int32)[None, :] < filled[:, None]
    pick_rows = jnp.take_along_axis(block_rows, chosen, axis=1)
    pick_cols = jnp.take_along_axis(block_cols, chosen, axis=1)
    pick_rows = jnp.where(live, pick_rows, device_ids[:, None])
    pick_cols = jnp.where(live, pick_cols, device_ids[:, None])
    all_rows = jnp.concatenate([device_ids[:, None], pick_rows], axis=1)
    all_cols = jnp.concatenate([device_ids[:, None], pick_cols], axis=1)
    all_live = jnp.concatenate([jnp.ones((DEVICES, 1), dtype=bool), live], axis=1)
    return (all_rows.reshape(-1), all_cols.reshape(-1), all_live.reshape(-1))


def draw_slot_row(key, part):
    row_ids, col_ids, live = pattern(key)
    return row_ids.astype(jnp.int32)


def draw_slot_col(key, part):
    row_ids, col_ids, live = pattern(key)
    return col_ids.astype(jnp.int32)


def draw_blocks(key, part):
    row_ids, col_ids, live = pattern(key)
    key = jax.random.fold_in(key, 11)
    noise_key, level_key = jax.random.split(key)
    shape = (DEVICES * SLOTS, BLOCK, BLOCK)
    noise = jax.random.normal(noise_key, shape, jnp.float32)
    tiles = noise * (0.07 / math.sqrt(BLOCK))
    symmetric = (tiles + jnp.swapaxes(tiles, 1, 2)) * (1.0 / math.sqrt(2.0))
    levels = 1.5 * 4.0 ** jax.random.uniform(level_key, (DEVICES * SLOTS, BLOCK), jnp.float32)
    identity = jnp.eye(BLOCK, dtype=jnp.float32)
    diag_tiles = symmetric + identity[None, :, :] * levels[:, :, None]
    is_diag = jnp.arange(DEVICES * SLOTS) % SLOTS == 0
    live_scale = live.astype(jnp.float32)
    return jnp.where(is_diag[:, None, None], diag_tiles, tiles * live_scale[:, None, None]).astype(jnp.float32)


def block_scale(own_key, shape, shards, low, top_value):
    level = 1.0
    for axis_at, blocks in shards:
        draws = jax.random.uniform(jax.random.fold_in(jax.random.fold_in(own_key, 6), axis_at), (blocks,), jnp.float32, low / len(shards), top_value / len(shards))
        level = level * jnp.repeat(jnp.exp(draws), shape[axis_at] // blocks).reshape((-1,) + (1,) * (len(shape) - 1 - axis_at))
    return level


def centred(key, extent, spread, limit, shards=(), kind=jnp.bfloat16):
    drawn = jax.random.normal(key, extent, jnp.float32) * spread
    if len(shards) > 0:
        drawn = block_scale(key, extent, shards, -0.22, 0.18) * drawn
    return jnp.clip(drawn, min=-limit, max=limit).astype(kind)


def setup_inputs(seed: int = 0) -> dict:
    key_of = jax.random.split(jax.random.key(seed), 5)
    return {
        "right_side": centred(key_of[0], (SIDES, ORDER), 1.0, 6.0, ((1, 256),), jnp.float32),
        "blocks": draw_blocks(jax.random.fold_in(key_of[4], 71), 0),
        "slot_row": draw_slot_row(jax.random.fold_in(key_of[4], 71), 0),
        "slot_col": draw_slot_col(jax.random.fold_in(key_of[4], 71), 0),
    }


def apply_matrix(direction, blocks, slot_row, slot_col):
    side_count = direction.shape[0]
    pieces = direction.reshape(side_count, NBLK, BLOCK)
    grouped = blocks.reshape(DEVICES, SLOTS, BLOCK, BLOCK)
    row_ids = slot_row.reshape(DEVICES, SLOTS).astype(jnp.int32)
    col_ids = slot_col.reshape(DEVICES, SLOTS).astype(jnp.int32)

    def add_group(accumulated, inputs):
        tile_group, row_here, col_here = inputs
        near_dirs = pieces[:, col_here, :]
        far_dirs = pieces[:, row_here, :]
        direct = jnp.einsum('rsb,sab->rsa', near_dirs, tile_group, precision=lax.Precision.HIGHEST)
        mirrored = jnp.einsum('rsa,sab->rsb', far_dirs, tile_group, precision=lax.Precision.HIGHEST)
        off_diagonal = (row_here != col_here).astype(jnp.float32)
        mirrored = mirrored * off_diagonal[None, :, None]
        accumulated = accumulated.at[:, row_here, :].add(direct)
        accumulated = accumulated.at[:, col_here, :].add(mirrored)
        return (accumulated, None)
    start_zero = jnp.zeros((side_count, NBLK, BLOCK), jnp.float32)
    accumulated, _ = lax.scan(add_group, start_zero, (grouped, row_ids, col_ids))
    return accumulated.reshape(side_count, NBLK * BLOCK)

def gram_matrix(first_vec, second_vec):
    return jnp.dot(first_vec, second_vec.T, precision=lax.Precision.HIGHEST)

def solve_small(matrix, right_hand):
    factor = jnp.linalg.cholesky(matrix)
    halfway = lax.linalg.triangular_solve(factor, right_hand, left_side=True, lower=True)
    return lax.linalg.triangular_solve(factor, halfway, left_side=True, lower=True, transpose_a=True)

def reference(right_side, blocks, slot_row, slot_col):
    solution = jnp.zeros_like(right_side)
    residual = right_side
    direction = right_side
    res_gram = gram_matrix(residual, residual)
    for iteration in range(ITERS):
        images = apply_matrix(direction, blocks, slot_row, slot_col)
        curvature = gram_matrix(direction, images)
        step_matrix = solve_small(curvature, res_gram)
        solution = solution + jnp.dot(step_matrix.T, direction, precision=lax.Precision.HIGHEST)
        residual = residual - jnp.dot(step_matrix.T, images, precision=lax.Precision.HIGHEST)
        if iteration + 1 < ITERS:
            new_gram = gram_matrix(residual, residual)
            mix_matrix = solve_small(res_gram, new_gram)
            direction = residual + jnp.dot(mix_matrix.T, direction, precision=lax.Precision.HIGHEST)
            res_gram = new_gram
    return (solution, residual)
```

```python
import jax
import jax.numpy as jnp
from jax import lax
from jax.experimental import pallas as pl
from jax.experimental.pallas import tpu as pltpu
from jax.sharding import Mesh, PartitionSpec as P

ITERS = 4
WIDTH = 512
HIGHEST = lax.Precision.HIGHEST
AXES = ("z", "y", "x", "c")
SIZES = {"z": 8, "y": 4, "x": 4, "c": 2}
F32 = jnp.float32
NN = (((1,), (0,)), ((), ()))
NT = (((1,), (1,)), ((), ()))
WHOLE = pl.BlockSpec(memory_space=pltpu.VMEM)


def rows_of(count):
    return jax.ShapeDtypeStruct((count, WIDTH), F32)


SMALL = jax.ShapeDtypeStruct((32, 32), F32)


def shift(value, axis, by):
    size = SIZES[axis]
    return lax.ppermute(value, axis, [(i, (i + by) % size) for i in range(size)])


def swap(value, axis, bit):
    return lax.ppermute(value, axis, [(i, i ^ bit) for i in range(SIZES[axis])])


def call(kernel, out_shape, *operands):
    return pl.pallas_call(
        kernel,
        in_specs=[WHOLE] * len(operands),
        out_specs=jax.tree.map(lambda _: WHOLE, out_shape),
        out_shape=out_shape,
        name=kernel.__name__,
    )(*operands)


def pack(matrix):
    return jnp.concatenate([matrix[8 * k : 8 * k + 8] for k in range(4)], axis=1)


def unpack(rows):
    return jnp.concatenate([rows[:, 32 * k : 32 * k + 32] for k in range(4)], axis=0)


def dot(left, right, dims=NN):
    return lax.dot_general(left, right, dims, precision=HIGHEST, preferred_element_type=F32)


def solve(matrix, right_hand):
    held = jnp.concatenate([matrix, right_hand], axis=1)
    row_id = lax.broadcasted_iota(jnp.int32, held.shape, 0)
    for k in range(32):
        row = held[k : k + 1] / held[k : k + 1, k : k + 1]
        held = jnp.where(row_id == k, row, held - held[:, k : k + 1] * row)
    return held[:, 32:]


def write_message(message_ref, residual, images):
    message_ref[0:32, :] = residual
    parts = [pack(dot(residual, residual, NT))]
    parts.append(jnp.zeros((8, 128), F32) if images is None else pack(dot(images, residual, NT)))
    parts.append(jnp.zeros((8, 256), F32))
    message_ref[32:40, :] = jnp.concatenate(parts, axis=1)


def first_kernel(residual_ref, message_ref):
    write_message(message_ref, residual_ref[...], None)


def mix_kernel(
    tail_ref, gram_ref, curvature_ref, images_ref, direction_ref, residual_ref,
    cross_ref, direction_out, images_out,
):
    new_gram = unpack(tail_ref[:, 0:128])
    outer = unpack(tail_ref[:, 128:256])
    mix_t = solve(gram_ref[...], new_gram).T
    cross = dot(mix_t, outer)
    bent = dot(dot(mix_t, curvature_ref[...]), mix_t, NT)
    cross_ref[...] = cross + cross.T + 0.5 * (bent + bent.T)
    direction_out[...] = residual_ref[...] + dot(mix_t, direction_ref[...])
    images_out[...] = dot(mix_t, images_ref[...])


def step_core(
    tail_ref, energy_ref, other_ref, near_ref, up_ref, down_ref, far_ref, column_ref, residual_ref,
):
    gram = unpack(tail_ref[:, 0:128])
    energy = unpack(energy_ref[...] + other_ref[...])
    product = column_ref[...] + (near_ref[...] + ((up_ref[...] + down_ref[...]) + far_ref[...]))
    return gram, energy + energy.T, product


def step_first_kernel(*refs):
    residual_ref = refs[8]
    solution_out, residual_out, images_out, message_out, gram_out, curvature_out = refs[9:]
    gram, curvature, images = step_core(*refs[:9])
    step_t = solve(curvature, gram).T
    residual = residual_ref[...]
    solution_out[...] = dot(step_t, residual)
    after = residual - dot(step_t, images)
    residual_out[...] = after
    images_out[...] = images
    write_message(message_out, after, images)
    gram_out[...] = gram
    curvature_out[...] = curvature


def step_kernel(*refs):
    residual_ref, cross_ref, direction_ref, images_ref, solution_ref = refs[8:13]
    solution_out, residual_out, images_out, message_out, gram_out, curvature_out = refs[13:]
    gram, energy, product = step_core(*refs[:9])
    curvature = energy + cross_ref[...]
    images = product + images_ref[...]
    step_t = solve(curvature, gram).T
    solution_out[...] = solution_ref[...] + dot(step_t, direction_ref[...])
    after = residual_ref[...] - dot(step_t, images)
    residual_out[...] = after
    images_out[...] = images
    write_message(message_out, after, images)
    gram_out[...] = gram
    curvature_out[...] = curvature


def halves(value):
    high = value.astype(jnp.bfloat16)
    low = (value - high.astype(F32)).astype(jnp.bfloat16)
    return high, low


def split_dot(left, right, dims):
    left_high, left_low = halves(left)
    right_high, right_low = halves(right)
    rows = left.shape[0]
    both = lax.dot_general(
        jnp.concatenate([left_high, left_low]), right_high, dims, preferred_element_type=F32
    )
    rest = lax.dot_general(left_high, right_low, dims, preferred_element_type=F32)
    return both[:rows] + (both[rows:] + rest)


def piece(ref, at):
    return ref[pl.ds(pl.multiple_of(at * 8, 8), 32), :]


def prepare_kernel(block_ref, out_ref):
    block = block_ref[0]
    out_ref[0, 0], out_ref[0, 1] = halves(block)
    out_ref[0, 2], out_ref[0, 3] = halves(block.T)


def prepare(blocks):
    return pl.pallas_call(
        prepare_kernel,
        grid=(blocks.shape[0],),
        in_specs=[pl.BlockSpec((1, 512, 512), lambda s: (s, 0, 0))],
        out_specs=pl.BlockSpec((1, 4, 512, 512), lambda s: (s, 0, 0, 0)),
        out_shape=jax.ShapeDtypeStruct((blocks.shape[0], 4, 512, 512), jnp.bfloat16),
        compiler_params=pltpu.CompilerParams(vmem_limit_bytes=32 << 20),
        name="prepare",
    )(blocks)


def fetch(pairs, sems):
    copies = [pltpu.make_async_copy(a, b, sems.at[k]) for k, (a, b) in enumerate(pairs)]
    for copy in copies:
        copy.start()
    return copies


def stacked(refs, target):
    pairs, at = [], 0
    for ref in refs:
        pairs.append((ref, target.at[at : at + ref.shape[0]]))
        at += ref.shape[0]
    return pairs


def block_product(rows, high, low):
    rows_high, rows_low = halves(rows)
    both = jnp.dot(jnp.concatenate([rows_high, rows_low]), high, preferred_element_type=F32)
    rest = jnp.dot(rows_high, low, preferred_element_type=F32)
    return both[:32] + (both[32:] + rest)


FIRST = 1


def mirrored_kernel(
    row_ref, to_ref, off_ref, half_ref, other_ref, split_hbm,
    out_ref, up_ref, down_ref, held_ref, split_ref, sems,
):
    slots = split_hbm.shape[0]
    pairs = stacked((half_ref, other_ref), held_ref)
    for s in range(FIRST, slots):
        pairs.append((split_hbm.at[s, 0:2], split_ref.at[s - FIRST]))
    copies = fetch(pairs, sems)
    out_ref[...] = jnp.zeros_like(out_ref)
    copies[0].wait()
    copies[1].wait()
    for s in range(FIRST, slots):
        k = s - FIRST
        copies[2 + k].wait()
        product = block_product(piece(held_ref, row_ref[s]), split_ref[k, 0], split_ref[k, 1])
        at = pl.ds(pl.multiple_of(to_ref[s] * 8, 8), 32)
        out_ref[at, :] += jnp.where(off_ref[s] == 1, product, 0.0)
    up_ref[...] = out_ref[896:960, :]
    down_ref[...] = out_ref[960:1024, :]


SCALARS = pl.BlockSpec(memory_space=pltpu.SMEM)
ANY = pl.BlockSpec(memory_space=pl.ANY)


def mirrored_products(held, split, row_at, to_at, off):
    slots = split.shape[0]
    return pl.pallas_call(
        mirrored_kernel,
        in_specs=[SCALARS] * 3 + [ANY] * 3,
        out_specs=[WHOLE] * 3,
        out_shape=[rows_of(1024), rows_of(64), rows_of(64)],
        scratch_shapes=[
            pltpu.VMEM((256, WIDTH), F32),
            pltpu.VMEM((slots - FIRST, 2, 512, 512), jnp.bfloat16),
            pltpu.SemaphoreType.DMA((2 + slots - FIRST,)),
        ],
        compiler_params=pltpu.CompilerParams(vmem_limit_bytes=44 << 20),
        cost_estimate=pl.CostEstimate(
            flops=2 * 11 * 64 * 512 * 512, bytes_accessed=15 << 20, transcendentals=0
        ),
        name="mirrored",
    )(row_at, to_at, off, *held, split)


def direct_kernel(row_ref, from_ref, half_ref, other_ref, *refs):
    groups, split_hbm = refs[:9], refs[9]
    sum_ref, tail_ref, near_ref, held_ref, diag_ref, split_ref, sems = refs[10:]
    slots = split_hbm.shape[0]
    pairs = stacked(groups, near_ref)
    for s in range(slots):
        pairs.append((split_hbm.at[s, 2:4], split_ref.at[s]))
    pairs += stacked((half_ref, other_ref), held_ref)
    copies = fetch(pairs, sems)
    sum_ref[...] = jnp.zeros_like(sum_ref)
    for k in range(9):
        copies[k].wait()
    for s in range(slots):
        copies[9 + s].wait()
        product = block_product(piece(near_ref, from_ref[s]), split_ref[s, 0], split_ref[s, 1])
        if s == 0:
            diag_ref[...] = product
        at = pl.ds(pl.multiple_of(row_ref[s] * 8, 8), 32)
        sum_ref[at, :] += product
    copies[-2].wait()
    copies[-1].wait()
    half = split_dot(held_ref[0:32, :], sum_ref[0:32, :] - 0.5 * diag_ref[...], NT)
    for k in range(1, 8):
        half += split_dot(held_ref[32 * k : 32 * k + 32, :], sum_ref[32 * k : 32 * k + 32, :], NT)
    tail = near_ref[128:136, :]
    for k in range(1, 8):
        tail += near_ref[136 * k + 128 : 136 * k + 136, :]
    tail_ref[...] = jnp.concatenate([tail[:, 0:256], pack(half), tail[:, 384:512]], axis=1)


def direct_products(held, groups, split, row_at, from_at):
    slots = split.shape[0]
    return pl.pallas_call(
        direct_kernel,
        in_specs=[SCALARS] * 2 + [ANY] * 12,
        out_specs=[WHOLE] * 2,
        out_shape=[rows_of(256), rows_of(8)],
        scratch_shapes=[
            pltpu.VMEM((1088, WIDTH), F32),
            pltpu.VMEM((256, WIDTH), F32),
            pltpu.VMEM((32, WIDTH), F32),
            pltpu.VMEM((slots, 2, 512, 512), jnp.bfloat16),
            pltpu.SemaphoreType.DMA((11 + slots,)),
        ],
        compiler_params=pltpu.CompilerParams(vmem_limit_bytes=44 << 20),
        cost_estimate=pl.CostEstimate(
            flops=2 * 12 * 64 * 512 * 512, bytes_accessed=15 << 20, transcendentals=0
        ),
        name="direct",
    )(row_at, from_at, *held, *groups, split)


def barrier(*values):
    return lax.optimization_barrier(values)


def local(right_side, blocks, slot_row, slot_col):
    z, y = lax.axis_index("z"), lax.axis_index("y")
    column = lax.axis_index("x") * 2 + lax.axis_index("c")
    row_at = ((slot_row % 8) ^ column) * 4
    target = slot_col // 8
    dz = (target // 4 - z) % 8
    dy = (target % 4 - y) % 4
    from_at = jnp.where(dz < 4, 2 * dz, 15 - 2 * dz) * 17 + jnp.where(dy == 0, 0, dy % 3 + 1) * 4
    to_z = jnp.where(dz == 0, 0, jnp.where(dz <= 4, 2 * dz - 1, 16 - 2 * dz))
    to_at = (to_z * 4 + jnp.where(dy < 2, dy, 5 - dy)) * 4
    off = (slot_row != slot_col).astype(jnp.int32)

    split = prepare(blocks)
    residual = right_side
    message = call(first_kernel, rows_of(40), right_side)
    solution = direction = images = gram = curvature = None
    for iteration in range(ITERS):
        got = (message, shift(message, "y", 1), shift(message, "y", -1), shift(message, "y", 2))
        first = swap(residual, "c", 1)
        *got, first = barrier(*got, first)
        tails = [part[32:40] for part in got]
        group = jnp.concatenate(
            [part[:32] for part in got] + [(tails[0] + tails[1]) + (tails[2] + tails[3])]
        )
        pair = jnp.concatenate([residual, first])
        group, pair = barrier(group, pair)
        up, down = shift(group, "z", 1), shift(group, "z", -1)
        got = swap(pair, "x", 1)
        up, down, got = barrier(up, down, got)
        groups = [group, up, down]
        quad = jnp.concatenate([pair, got])
        up, down = shift(up, "z", 1), shift(down, "z", -1)
        other = swap(quad, "x", 2)
        up, down, other = barrier(up, down, other)
        groups += [up, down]
        held = (quad, other)
        up, down = shift(up, "z", 1), shift(down, "z", -1)
        spread, go_up, go_down = mirrored_products(held, split, row_at, to_at, off)
        up, down, go_up, go_down = barrier(up, down, go_up, go_down)
        groups += [up, down]
        groups += [shift(up[:64], "z", 1), shift(down[64:], "z", -1)]
        up, down = shift(go_up, "z", 1), shift(go_down, "z", -1)
        *groups, up, down = barrier(*groups, up, down)
        up = jnp.concatenate([spread[640:704] + up, spread[704:768]])
        down = jnp.concatenate([spread[768:832], spread[832:896] + down])
        up, down, *groups = barrier(up, down, *groups)
        up, down = shift(up, "z", 1), shift(down, "z", -1)
        summed, tail = direct_products(held, groups, split, row_at, from_at)

        tail = tail + swap(tail, "c", 1)
        tail = tail + swap(tail, "x", 1)
        up, down, tail = barrier(up, down, tail)
        up, down = spread[384:512] + up, spread[512:640] + down
        up, down, tail = barrier(up, down, tail)
        up, down = shift(up, "z", 1), shift(down, "z", -1)
        four = summed[:128] + swap(summed[128:], "x", 2)
        tail = tail + swap(tail, "x", 2)
        energy = tail[:, 256:384]
        energy = energy + swap(energy, "y", 1)
        up, down, energy, four = barrier(up, down, energy, four)
        up, down = spread[128:256] + up, spread[256:384] + down
        up, down, energy = barrier(up, down, energy)
        up, down = shift(up, "z", 1), shift(down, "z", -1)
        two = four[:64] + swap(four[64:], "x", 1)
        energy = energy + swap(energy, "y", 2)
        energy = energy + swap(energy, "z", 1)
        up, down, energy, two = barrier(up, down, energy, two)
        near, up, down, far = jnp.split(spread[0:128] + (up + down), 4)
        near, up, down, far, energy = barrier(near, up, down, far, energy)
        up, down, far = shift(up, "y", 1), shift(down, "y", -1), shift(far, "y", 2)
        column_part = two[:32] + swap(two[32:], "c", 1)
        energy = energy + swap(energy, "z", 2)
        if iteration > 0:
            cross, direction, images = call(
                mix_kernel, [SMALL, rows_of(32), rows_of(32)],
                tail, gram, curvature, images, direction, residual,
            )
        core = (tail, energy, swap(energy, "z", 4), near, up, down, far, column_part, residual)
        outs = [rows_of(32), rows_of(32), rows_of(32), rows_of(40), SMALL, SMALL]
        if iteration == 0:
            direction = residual
            solution, residual, images, message, gram, curvature = call(
                step_first_kernel, outs, *core
            )
        else:
            solution, residual, images, message, gram, curvature = call(
                step_kernel, outs, *core, cross, direction, images, solution
            )
    return (solution, residual)


def solution(mesh):
    fine = Mesh(mesh.devices.reshape(8, 4, 4, 2), AXES)
    return jax.shard_map(
        local,
        mesh=fine,
        in_specs=(P(None, AXES), P(AXES, None, None), P(AXES), P(AXES)),
        out_specs=(P(None, AXES), P(None, AXES)),
        check_vma=False,
    )
```

```python
import jax
import jax.numpy as jnp
from jax import lax
from jax.experimental import pallas as pl
from jax.experimental.pallas import tpu as pltpu
from jax.sharding import Mesh, PartitionSpec as P

ITERS = 4
WIDTH = 512
HIGHEST = lax.Precision.HIGHEST
AXES = ("z", "y", "x", "c")
SIZES = {"z": 8, "y": 4, "x": 4, "c": 2}
F32 = jnp.float32
NN = (((1,), (0,)), ((), ()))
NT = (((1,), (1,)), ((), ()))
WHOLE = pl.BlockSpec(memory_space=pltpu.VMEM)


def rows_of(count):
    return jax.ShapeDtypeStruct((count, WIDTH), F32)


SMALL = jax.ShapeDtypeStruct((32, 32), F32)


def shift(value, axis, by):
    size = SIZES[axis]
    return lax.ppermute(value, axis, [(i, (i + by) % size) for i in range(size)])


def swap(value, axis, bit):
    return lax.ppermute(value, axis, [(i, i ^ bit) for i in range(SIZES[axis])])


def around(value, axis):
    return shift(value, axis, 1), shift(value, axis, -1), shift(value, axis, 2)


def call(kernel, out_shape, *operands):
    return pl.pallas_call(
        kernel,
        in_specs=[WHOLE] * len(operands),
        out_specs=jax.tree.map(lambda _: WHOLE, out_shape),
        out_shape=out_shape,
        name=kernel.__name__,
    )(*operands)


def pack(matrix):
    return jnp.concatenate([matrix[8 * k : 8 * k + 8] for k in range(4)], axis=1)


def unpack(rows):
    return jnp.concatenate([rows[:, 32 * k : 32 * k + 32] for k in range(4)], axis=0)


def dot(left, right, dims=NN):
    return lax.dot_general(left, right, dims, precision=HIGHEST, preferred_element_type=F32)


def solve(matrix, right_hand):
    held = jnp.concatenate([matrix, right_hand], axis=1)
    row_id = lax.broadcasted_iota(jnp.int32, held.shape, 0)
    for k in range(32):
        row = held[k : k + 1] / held[k : k + 1, k : k + 1]
        held = jnp.where(row_id == k, row, held - held[:, k : k + 1] * row)
    return held[:, 32:]


def write_message(message_ref, residual, images):
    message_ref[0:32, :] = residual
    parts = [pack(dot(residual, residual, NT))]
    parts.append(jnp.zeros((8, 128), F32) if images is None else pack(dot(images, residual, NT)))
    parts.append(jnp.zeros((8, 256), F32))
    message_ref[32:40, :] = jnp.concatenate(parts, axis=1)


def first_kernel(residual_ref, message_ref):
    write_message(message_ref, residual_ref[...], None)


def mix_kernel(
    tail_ref, gram_ref, curvature_ref, images_ref, direction_ref, residual_ref,
    cross_ref, direction_out, images_out,
):
    new_gram = unpack(tail_ref[:, 0:128])
    outer = unpack(tail_ref[:, 128:256])
    mix_t = solve(gram_ref[...], new_gram).T
    cross = dot(mix_t, outer)
    bent = dot(dot(mix_t, curvature_ref[...]), mix_t, NT)
    cross_ref[...] = cross + cross.T + 0.5 * (bent + bent.T)
    direction_out[...] = residual_ref[...] + dot(mix_t, direction_ref[...])
    images_out[...] = dot(mix_t, images_ref[...])


def step_core(
    tail_ref, energy_ref, other_ref, near_ref, up_ref, down_ref, far_ref, column_ref, residual_ref,
):
    gram = unpack(tail_ref[:, 0:128])
    energy = unpack(energy_ref[...] + other_ref[...])
    product = column_ref[...] + (near_ref[...] + ((up_ref[...] + down_ref[...]) + far_ref[...]))
    return gram, energy + energy.T, product


def step_first_kernel(*refs):
    residual_ref = refs[8]
    solution_out, residual_out, images_out, message_out, gram_out, curvature_out = refs[9:]
    gram, curvature, images = step_core(*refs[:9])
    step_t = solve(curvature, gram).T
    residual = residual_ref[...]
    solution_out[...] = dot(step_t, residual)
    after = residual - dot(step_t, images)
    residual_out[...] = after
    images_out[...] = images
    write_message(message_out, after, images)
    gram_out[...] = gram
    curvature_out[...] = curvature


def step_kernel(*refs):
    residual_ref, cross_ref, direction_ref, images_ref, solution_ref = refs[8:13]
    solution_out, residual_out, images_out, message_out, gram_out, curvature_out = refs[13:]
    gram, energy, product = step_core(*refs[:9])
    curvature = energy + cross_ref[...]
    images = product + images_ref[...]
    step_t = solve(curvature, gram).T
    solution_out[...] = solution_ref[...] + dot(step_t, direction_ref[...])
    after = residual_ref[...] - dot(step_t, images)
    residual_out[...] = after
    images_out[...] = images
    write_message(message_out, after, images)
    gram_out[...] = gram
    curvature_out[...] = curvature


def halves(value):
    high = value.astype(jnp.bfloat16)
    low = (value - high.astype(F32)).astype(jnp.bfloat16)
    return high, low


def split_dot(left, right, dims):
    left_high, left_low = halves(left)
    right_high, right_low = halves(right)
    rows = left.shape[0]
    both = lax.dot_general(
        jnp.concatenate([left_high, left_low]), right_high, dims, preferred_element_type=F32
    )
    rest = lax.dot_general(left_high, right_low, dims, preferred_element_type=F32)
    return both[:rows] + (both[rows:] + rest)


def piece(ref, at):
    return ref[pl.ds(pl.multiple_of(at * 8, 8), 32), :]


def prepare_kernel(block_ref, out_ref):
    block = block_ref[0]
    out_ref[0, 0], out_ref[0, 1] = halves(block)
    out_ref[0, 2], out_ref[0, 3] = halves(block.T)


def prepare(blocks):
    return pl.pallas_call(
        prepare_kernel,
        grid=(blocks.shape[0],),
        in_specs=[pl.BlockSpec((1, 512, 512), lambda s: (s, 0, 0))],
        out_specs=pl.BlockSpec((1, 4, 512, 512), lambda s: (s, 0, 0, 0)),
        out_shape=jax.ShapeDtypeStruct((blocks.shape[0], 4, 512, 512), jnp.bfloat16),
        compiler_params=pltpu.CompilerParams(vmem_limit_bytes=32 << 20),
        name="prepare",
    )(blocks)


def fetch(pairs, sems):
    copies = [pltpu.make_async_copy(a, b, sems.at[k]) for k, (a, b) in enumerate(pairs)]
    for copy in copies:
        copy.start()
    return copies


def stacked(refs, target):
    pairs, at = [], 0
    for ref in refs:
        pairs.append((ref, target.at[at : at + ref.shape[0]]))
        at += ref.shape[0]
    return pairs


def block_product(rows, high, low):
    rows_high, rows_low = halves(rows)
    both = jnp.dot(jnp.concatenate([rows_high, rows_low]), high, preferred_element_type=F32)
    rest = jnp.dot(rows_high, low, preferred_element_type=F32)
    return both[:32] + (both[32:] + rest)


FIRST = 1


def mirrored_kernel(
    row_ref, to_ref, off_ref, pair_0, pair_1, pair_2, pair_3, split_hbm,
    out_ref, up_ref, down_ref, held_ref, split_ref, sems,
):
    slots = split_hbm.shape[0]
    pairs = stacked((pair_0, pair_1, pair_2, pair_3), held_ref)
    for s in range(FIRST, slots):
        pairs.append((split_hbm.at[s, 0:2], split_ref.at[s - FIRST]))
    copies = fetch(pairs, sems)
    out_ref[...] = jnp.zeros_like(out_ref)
    for k in range(4):
        copies[k].wait()
    for s in range(FIRST, slots):
        k = s - FIRST
        copies[4 + k].wait()
        product = block_product(piece(held_ref, row_ref[s]), split_ref[k, 0], split_ref[k, 1])
        at = pl.ds(pl.multiple_of(to_ref[s] * 8, 8), 32)
        out_ref[at, :] += jnp.where(off_ref[s] == 1, product, 0.0)
    up_ref[...] = out_ref[896:960, :]
    down_ref[...] = out_ref[960:1024, :]


SCALARS = pl.BlockSpec(memory_space=pltpu.SMEM)
ANY = pl.BlockSpec(memory_space=pl.ANY)


def mirrored_products(held, split, row_at, to_at, off):
    slots = split.shape[0]
    return pl.pallas_call(
        mirrored_kernel,
        in_specs=[SCALARS] * 3 + [ANY] * 5,
        out_specs=[WHOLE] * 3,
        out_shape=[rows_of(1024), rows_of(64), rows_of(64)],
        scratch_shapes=[
            pltpu.VMEM((256, WIDTH), F32),
            pltpu.VMEM((slots - FIRST, 2, 512, 512), jnp.bfloat16),
            pltpu.SemaphoreType.DMA((4 + slots - FIRST,)),
        ],
        compiler_params=pltpu.CompilerParams(vmem_limit_bytes=44 << 20),
        cost_estimate=pl.CostEstimate(
            flops=2 * 11 * 64 * 512 * 512, bytes_accessed=15 << 20, transcendentals=0
        ),
        name="mirrored",
    )(row_at, to_at, off, *held, split)


def direct_kernel(row_ref, from_ref, place_ref, pair_0, pair_1, pair_2, pair_3, *refs):
    groups, split_hbm = refs[:9], refs[9]
    sum_ref, tail_ref, near_ref, held_ref, diag_ref, split_ref, sems = refs[10:]
    slots = split_hbm.shape[0]
    pairs = stacked(groups, near_ref)
    for s in range(slots):
        pairs.append((split_hbm.at[s, 2:4], split_ref.at[s]))
    pairs += stacked((pair_0, pair_1, pair_2, pair_3), held_ref)
    copies = fetch(pairs, sems)
    sum_ref[...] = jnp.zeros_like(sum_ref)
    for k in range(9):
        copies[k].wait()
    for s in range(slots):
        copies[9 + s].wait()
        product = block_product(piece(near_ref, from_ref[s]), split_ref[s, 0], split_ref[s, 1])
        if s == 0:
            diag_ref[...] = product
        at = pl.ds(pl.multiple_of(row_ref[s] * 8, 8), 32)
        sum_ref[at, :] += product
    for k in range(9 + slots, 13 + slots):
        copies[k].wait()
    half = split_dot(held_ref[0:32, :], sum_ref[0:32, :] - 0.5 * diag_ref[...], NT)
    for k in range(1, 8):
        half += split_dot(piece(held_ref, place_ref[k]), sum_ref[32 * k : 32 * k + 32, :], NT)
    tail = near_ref[128:136, :]
    for k in range(1, 8):
        tail += near_ref[136 * k + 128 : 136 * k + 136, :]
    tail_ref[...] = jnp.concatenate([tail[:, 0:256], pack(half), tail[:, 384:512]], axis=1)


def direct_products(held, groups, split, row_at, from_at, place):
    slots = split.shape[0]
    return pl.pallas_call(
        direct_kernel,
        in_specs=[SCALARS] * 3 + [ANY] * 14,
        out_specs=[WHOLE] * 2,
        out_shape=[rows_of(256), rows_of(8)],
        scratch_shapes=[
            pltpu.VMEM((1088, WIDTH), F32),
            pltpu.VMEM((256, WIDTH), F32),
            pltpu.VMEM((32, WIDTH), F32),
            pltpu.VMEM((slots, 2, 512, 512), jnp.bfloat16),
            pltpu.SemaphoreType.DMA((13 + slots,)),
        ],
        compiler_params=pltpu.CompilerParams(vmem_limit_bytes=44 << 20),
        cost_estimate=pl.CostEstimate(
            flops=2 * 12 * 64 * 512 * 512, bytes_accessed=15 << 20, transcendentals=0
        ),
        name="direct",
    )(row_at, from_at, place, *held, *groups, split)


def barrier(*values):
    return lax.optimization_barrier(values)


def local(right_side, blocks, slot_row, slot_col):
    z, y = lax.axis_index("z"), lax.axis_index("y")
    x, c = lax.axis_index("x"), lax.axis_index("c")
    sum_at = ((slot_row % 8) ^ (2 * x + c)) * 4

    def held_place(column):
        dx = (column // 2 - x) % 4
        return (jnp.where(dx == 0, 0, dx % 3 + 1) * 2 + (column % 2 ^ c)) * 4

    row_at = held_place(slot_row % 8)
    place = held_place(jnp.arange(8, dtype=jnp.int32) ^ (2 * x + c))
    target = slot_col // 8
    dz = (target // 4 - z) % 8
    dy = (target % 4 - y) % 4
    from_at = jnp.where(dz < 4, 2 * dz, 15 - 2 * dz) * 17 + jnp.where(dy == 0, 0, dy % 3 + 1) * 4
    to_z = jnp.where(dz == 0, 0, jnp.where(dz <= 4, 2 * dz - 1, 16 - 2 * dz))
    to_at = (to_z * 4 + jnp.where(dy < 2, dy, 5 - dy)) * 4
    off = (slot_row != slot_col).astype(jnp.int32)

    residual = right_side
    message = call(first_kernel, rows_of(40), right_side)
    solution = direction = images = gram = curvature = split = None
    for iteration in range(ITERS):
        got = (message, *around(message, "y"))
        first = swap(residual, "c", 1)
        *got, first = barrier(*got, first)
        tails = [part[32:40] for part in got]
        group = jnp.concatenate(
            [part[:32] for part in got] + [(tails[0] + tails[1]) + (tails[2] + tails[3])]
        )
        pair = jnp.concatenate([residual, first])
        group, pair = barrier(group, pair)
        up, down = shift(group, "z", 1), shift(group, "z", -1)
        held = around(pair, "x")
        if iteration == 0:
            split = prepare(blocks)
        up, down, split, *held = barrier(up, down, split, *held)
        groups = [group, up, down]
        up, down = shift(up, "z", 1), shift(down, "z", -1)
        spread, go_up, go_down = mirrored_products((pair, *held), split, row_at, to_at, off)
        up, down, go_up, go_down = barrier(up, down, go_up, go_down)
        groups += [up, down]
        up, down = shift(up, "z", 1), shift(down, "z", -1)
        go_up, go_down = shift(go_up, "z", 1), shift(go_down, "z", -1)
        up, down, go_up, go_down = barrier(up, down, go_up, go_down)
        groups += [up, down]
        up, down = shift(up[:64], "z", 1), shift(down[64:], "z", -1)
        go_up = jnp.concatenate([spread[640:704] + go_up, spread[704:768]])
        go_down = jnp.concatenate([spread[768:832], spread[832:896] + go_down])
        groups += [up, down]
        go_up, go_down, *groups = barrier(go_up, go_down, *groups)
        go_up, go_down = shift(go_up, "z", 1), shift(go_down, "z", -1)
        summed, tail = direct_products((pair, *held), groups, split, sum_at, from_at, place)

        tail = tail + swap(tail, "c", 1)
        go_up, go_down, tail = barrier(go_up, go_down, tail)
        go_up, go_down = spread[384:512] + go_up, spread[512:640] + go_down
        go_up, go_down, tail = barrier(go_up, go_down, tail)
        go_up, go_down = shift(go_up, "z", 1), shift(go_down, "z", -1)
        tail = tail + swap(tail, "x", 1)
        tail = tail + swap(tail, "x", 2)
        four = summed[:128] + swap(summed[128:], "x", 2)
        go_up, go_down, tail, four = barrier(go_up, go_down, tail, four)
        go_up, go_down = spread[128:256] + go_up, spread[256:384] + go_down
        go_up, go_down, tail = barrier(go_up, go_down, tail)
        energy = tail[:, 256:384]
        go_up, go_down = shift(go_up, "z", 1), shift(go_down, "z", -1)
        energy = energy + swap(energy, "y", 1)
        energy = energy + swap(energy, "y", 2)
        two = four[:64] + swap(four[64:], "x", 1)
        go_up, go_down, energy, two = barrier(go_up, go_down, energy, two)
        near, up, down, far = jnp.split(spread[0:128] + (go_up + go_down), 4)
        near, up, down, far, energy = barrier(near, up, down, far, energy)
        up, down, far = shift(up, "y", 1), shift(down, "y", -1), shift(far, "y", 2)
        column_part = two[:32] + swap(two[32:], "c", 1)
        energy = energy + swap(energy, "z", 1)
        energy = energy + swap(energy, "z", 2)
        if iteration > 0:
            cross, direction, images = call(
                mix_kernel, [SMALL, rows_of(32), rows_of(32)],
                tail, gram, curvature, images, direction, residual,
            )
        core = (tail, energy, swap(energy, "z", 4), near, up, down, far, column_part, residual)
        outs = [rows_of(32), rows_of(32), rows_of(32), rows_of(40), SMALL, SMALL]
        if iteration == 0:
            direction = residual
            solution, residual, images, message, gram, curvature = call(
                step_first_kernel, outs, *core
            )
        else:
            solution, residual, images, message, gram, curvature = call(
                step_kernel, outs, *core, cross, direction, images, solution
            )
    return (solution, residual)


def solution(mesh):
    fine = Mesh(mesh.devices.reshape(8, 4, 4, 2), AXES)
    return jax.shard_map(
        local,
        mesh=fine,
        in_specs=(P(None, AXES), P(AXES, None, None), P(AXES), P(AXES)),
        out_specs=(P(None, AXES), P(None, AXES)),
        check_vma=False,
    )
```

```python
import jax
import jax.numpy as jnp
from jax import lax
from jax.experimental import pallas as pl
from jax.experimental.pallas import tpu as pltpu
from jax.sharding import Mesh, PartitionSpec as P

ITERS = 4
WIDTH = 512
HIGHEST = lax.Precision.HIGHEST
AXES = ("z", "y", "x", "c")
SIZES = {"z": 8, "y": 4, "x": 4, "c": 2}
F32 = jnp.float32
NN = (((1,), (0,)), ((), ()))
NT = (((1,), (1,)), ((), ()))
WHOLE = pl.BlockSpec(memory_space=pltpu.VMEM)


def rows_of(count):
    return jax.ShapeDtypeStruct((count, WIDTH), F32)


SMALL = jax.ShapeDtypeStruct((32, 32), F32)


def shift(value, axis, by):
    size = SIZES[axis]
    return lax.ppermute(value, axis, [(i, (i + by) % size) for i in range(size)])


def swap(value, axis, bit):
    return lax.ppermute(value, axis, [(i, i ^ bit) for i in range(SIZES[axis])])


def around(value, axis):
    return shift(value, axis, 1), shift(value, axis, -1), shift(value, axis, 2)


def call(kernel, out_shape, *operands):
    return pl.pallas_call(
        kernel,
        in_specs=[WHOLE] * len(operands),
        out_specs=jax.tree.map(lambda _: WHOLE, out_shape),
        out_shape=out_shape,
        name=kernel.__name__,
    )(*operands)


def pack(matrix):
    return jnp.concatenate([matrix[8 * k : 8 * k + 8] for k in range(4)], axis=1)


def unpack(rows):
    return jnp.concatenate([rows[:, 32 * k : 32 * k + 32] for k in range(4)], axis=0)


def dot(left, right, dims=NN):
    return lax.dot_general(left, right, dims, precision=HIGHEST, preferred_element_type=F32)


def solve(matrix, right_hand):
    held = jnp.concatenate([matrix, right_hand], axis=1)
    row_id = lax.broadcasted_iota(jnp.int32, held.shape, 0)
    for k in range(32):
        row = held[k : k + 1] / held[k : k + 1, k : k + 1]
        held = jnp.where(row_id == k, row, held - held[:, k : k + 1] * row)
    return held[:, 32:]


def write_message(message_ref, residual, images):
    message_ref[0:32, :] = residual
    parts = [pack(dot(residual, residual, NT))]
    parts.append(jnp.zeros((8, 128), F32) if images is None else pack(dot(images, residual, NT)))
    parts.append(jnp.zeros((8, 256), F32))
    message_ref[32:40, :] = jnp.concatenate(parts, axis=1)


def first_kernel(residual_ref, message_ref):
    write_message(message_ref, residual_ref[...], None)


def mix_kernel(
    tail_ref, gram_ref, curvature_ref, images_ref, direction_ref, residual_ref,
    cross_ref, direction_out, images_out,
):
    new_gram = unpack(tail_ref[:, 0:128])
    outer = unpack(tail_ref[:, 128:256])
    mix_t = solve(gram_ref[...], new_gram).T
    cross = dot(mix_t, outer)
    bent = dot(dot(mix_t, curvature_ref[...]), mix_t, NT)
    cross_ref[...] = cross + cross.T + 0.5 * (bent + bent.T)
    direction_out[...] = residual_ref[...] + dot(mix_t, direction_ref[...])
    images_out[...] = dot(mix_t, images_ref[...])


def step_core(
    tail_ref, energy_ref, other_ref, near_ref, up_ref, down_ref, far_ref, column_ref, residual_ref,
):
    gram = unpack(tail_ref[:, 0:128])
    energy = unpack(energy_ref[...] + other_ref[...])
    product = column_ref[...] + (near_ref[...] + ((up_ref[...] + down_ref[...]) + far_ref[...]))
    return gram, energy + energy.T, product


def step_first_kernel(*refs):
    residual_ref = refs[8]
    solution_out, residual_out, images_out, message_out, gram_out, curvature_out = refs[9:]
    gram, curvature, images = step_core(*refs[:9])
    step_t = solve(curvature, gram).T
    residual = residual_ref[...]
    solution_out[...] = dot(step_t, residual)
    after = residual - dot(step_t, images)
    residual_out[...] = after
    images_out[...] = images
    write_message(message_out, after, images)
    gram_out[...] = gram
    curvature_out[...] = curvature


def step_kernel(*refs):
    residual_ref, cross_ref, direction_ref, images_ref, solution_ref = refs[8:13]
    solution_out, residual_out, images_out, message_out, gram_out, curvature_out = refs[13:]
    gram, energy, product = step_core(*refs[:9])
    curvature = energy + cross_ref[...]
    images = product + images_ref[...]
    step_t = solve(curvature, gram).T
    solution_out[...] = solution_ref[...] + dot(step_t, direction_ref[...])
    after = residual_ref[...] - dot(step_t, images)
    residual_out[...] = after
    images_out[...] = images
    write_message(message_out, after, images)
    gram_out[...] = gram
    curvature_out[...] = curvature


def halves(value):
    high = value.astype(jnp.bfloat16)
    low = (value - high.astype(F32)).astype(jnp.bfloat16)
    return high, low


def split_dot(left, right, dims):
    left_high, left_low = halves(left)
    right_high, right_low = halves(right)
    rows = left.shape[0]
    both = lax.dot_general(
        jnp.concatenate([left_high, left_low]), right_high, dims, preferred_element_type=F32
    )
    rest = lax.dot_general(left_high, right_low, dims, preferred_element_type=F32)
    return both[:rows] + (both[rows:] + rest)


def piece(ref, at):
    return ref[pl.ds(pl.multiple_of(at * 8, 8), 32), :]


def prepare_kernel(block_ref, out_ref):
    block = block_ref[0]
    out_ref[0, 0], out_ref[0, 1] = halves(block)
    out_ref[0, 2], out_ref[0, 3] = halves(block.T)


def prepare(blocks):
    return pl.pallas_call(
        prepare_kernel,
        grid=(blocks.shape[0],),
        in_specs=[pl.BlockSpec((1, 512, 512), lambda s: (s, 0, 0))],
        out_specs=pl.BlockSpec((1, 4, 512, 512), lambda s: (s, 0, 0, 0)),
        out_shape=jax.ShapeDtypeStruct((blocks.shape[0], 4, 512, 512), jnp.bfloat16),
        compiler_params=pltpu.CompilerParams(vmem_limit_bytes=32 << 20),
        name="prepare",
    )(blocks)


def fetch(pairs, sems):
    copies = [pltpu.make_async_copy(a, b, sems.at[k]) for k, (a, b) in enumerate(pairs)]
    for copy in copies:
        copy.start()
    return copies


def stacked(refs, target):
    pairs, at = [], 0
    for ref in refs:
        pairs.append((ref, target.at[at : at + ref.shape[0]]))
        at += ref.shape[0]
    return pairs


def block_product(rows, high, low):
    rows_high, rows_low = halves(rows)
    both = jnp.dot(jnp.concatenate([rows_high, rows_low]), high, preferred_element_type=F32)
    rest = jnp.dot(rows_high, low, preferred_element_type=F32)
    return both[:32] + (both[32:] + rest)


FIRST = 1


def mirrored_kernel(
    row_ref, to_ref, off_ref, pair_0, pair_1, pair_2, pair_3, split_hbm,
    out_ref, up_ref, down_ref, held_ref, split_ref, sems,
):
    slots = split_hbm.shape[0]
    pairs = stacked((pair_0, pair_1, pair_2, pair_3), held_ref)
    for s in range(FIRST, slots):
        pairs.append((split_hbm.at[s, 0:2], split_ref.at[s - FIRST]))
    copies = fetch(pairs, sems)
    out_ref[...] = jnp.zeros_like(out_ref)
    for k in range(4):
        copies[k].wait()
    for s in range(FIRST, slots):
        k = s - FIRST
        copies[4 + k].wait()
        product = block_product(piece(held_ref, row_ref[s]), split_ref[k, 0], split_ref[k, 1])
        at = pl.ds(pl.multiple_of(to_ref[s] * 8, 8), 32)
        out_ref[at, :] += jnp.where(off_ref[s] == 1, product, 0.0)
    up_ref[...] = out_ref[896:960, :]
    down_ref[...] = out_ref[960:1024, :]


SCALARS = pl.BlockSpec(memory_space=pltpu.SMEM)
ANY = pl.BlockSpec(memory_space=pl.ANY)


def mirrored_products(held, split, row_at, to_at, off):
    slots = split.shape[0]
    return pl.pallas_call(
        mirrored_kernel,
        in_specs=[SCALARS] * 3 + [ANY] * 5,
        out_specs=[WHOLE] * 3,
        out_shape=[rows_of(1024), rows_of(64), rows_of(64)],
        scratch_shapes=[
            pltpu.VMEM((256, WIDTH), F32),
            pltpu.VMEM((slots - FIRST, 2, 512, 512), jnp.bfloat16),
            pltpu.SemaphoreType.DMA((4 + slots - FIRST,)),
        ],
        compiler_params=pltpu.CompilerParams(vmem_limit_bytes=44 << 20),
        cost_estimate=pl.CostEstimate(
            flops=2 * 11 * 64 * 512 * 512, bytes_accessed=15 << 20, transcendentals=0
        ),
        name="mirrored",
    )(row_at, to_at, off, *held, split)


def direct_kernel(row_ref, from_ref, place_ref, pair_0, pair_1, pair_2, pair_3, *refs):
    groups, split_hbm = refs[:9], refs[9]
    sum_ref, tail_ref, near_ref, held_ref, diag_ref, split_ref, sems = refs[10:]
    slots = split_hbm.shape[0]
    pairs = stacked(groups, near_ref)
    for s in range(slots):
        pairs.append((split_hbm.at[s, 2:4], split_ref.at[s]))
    pairs += stacked((pair_0, pair_1, pair_2, pair_3), held_ref)
    copies = fetch(pairs, sems)
    sum_ref[...] = jnp.zeros_like(sum_ref)
    for k in range(9):
        copies[k].wait()
    for s in range(slots):
        copies[9 + s].wait()
        product = block_product(piece(near_ref, from_ref[s]), split_ref[s, 0], split_ref[s, 1])
        if s == 0:
            diag_ref[...] = product
        at = pl.ds(pl.multiple_of(row_ref[s] * 8, 8), 32)
        sum_ref[at, :] += product
    for k in range(9 + slots, 13 + slots):
        copies[k].wait()
    half = split_dot(held_ref[0:32, :], sum_ref[0:32, :] - 0.5 * diag_ref[...], NT)
    for k in range(1, 8):
        half += split_dot(piece(held_ref, place_ref[k]), sum_ref[32 * k : 32 * k + 32, :], NT)
    tail = near_ref[128:136, :]
    for k in range(1, 8):
        tail += near_ref[136 * k + 128 : 136 * k + 136, :]
    tail_ref[...] = jnp.concatenate([tail[:, 0:256], pack(half), tail[:, 384:512]], axis=1)


def direct_products(held, groups, split, row_at, from_at, place):
    slots = split.shape[0]
    return pl.pallas_call(
        direct_kernel,
        in_specs=[SCALARS] * 3 + [ANY] * 14,
        out_specs=[WHOLE] * 2,
        out_shape=[rows_of(256), rows_of(8)],
        scratch_shapes=[
            pltpu.VMEM((1088, WIDTH), F32),
            pltpu.VMEM((256, WIDTH), F32),
            pltpu.VMEM((32, WIDTH), F32),
            pltpu.VMEM((slots, 2, 512, 512), jnp.bfloat16),
            pltpu.SemaphoreType.DMA((13 + slots,)),
        ],
        compiler_params=pltpu.CompilerParams(vmem_limit_bytes=44 << 20),
        cost_estimate=pl.CostEstimate(
            flops=2 * 12 * 64 * 512 * 512, bytes_accessed=15 << 20, transcendentals=0
        ),
        name="direct",
    )(row_at, from_at, place, *held, *groups, split)


def barrier(*values):
    return lax.optimization_barrier(values)


def local(right_side, blocks, slot_row, slot_col):
    z, y = lax.axis_index("z"), lax.axis_index("y")
    x, c = lax.axis_index("x"), lax.axis_index("c")
    sum_at = ((slot_row % 8) ^ (2 * x + c)) * 4

    def held_place(column):
        dx = (column // 2 - x) % 4
        return (jnp.where(dx == 0, 0, dx % 3 + 1) * 2 + (column % 2 ^ c)) * 4

    row_at = held_place(slot_row % 8)
    place = held_place(jnp.arange(8, dtype=jnp.int32) ^ (2 * x + c))
    target = slot_col // 8
    dz = (target // 4 - z) % 8
    dy = (target % 4 - y) % 4
    from_at = jnp.where(dz < 4, 2 * dz, 15 - 2 * dz) * 17 + jnp.where(dy == 0, 0, dy % 3 + 1) * 4
    to_z = jnp.where(dz == 0, 0, jnp.where(dz <= 4, 2 * dz - 1, 16 - 2 * dz))
    to_at = (to_z * 4 + jnp.where(dy < 2, dy, 5 - dy)) * 4
    off = (slot_row != slot_col).astype(jnp.int32)

    residual = right_side
    message = call(first_kernel, rows_of(40), right_side)
    solution = direction = images = gram = curvature = split = None
    for iteration in range(ITERS):
        got = (message, *around(message, "y"))
        first = swap(residual, "c", 1)
        *got, first = barrier(*got, first)
        tails = [part[32:40] for part in got]
        group = jnp.concatenate(
            [part[:32] for part in got] + [(tails[0] + tails[1]) + (tails[2] + tails[3])]
        )
        pair = jnp.concatenate([residual, first])
        group, pair = barrier(group, pair)
        up, down = shift(group, "z", 1), shift(group, "z", -1)
        held = around(pair, "x")
        if iteration == 0:
            split = prepare(blocks)
        up, down, split, *held = barrier(up, down, split, *held)
        groups = [group, up, down]
        up, down = shift(up, "z", 1), shift(down, "z", -1)
        spread, go_up, go_down = mirrored_products((pair, *held), split, row_at, to_at, off)
        up, down, go_up, go_down = barrier(up, down, go_up, go_down)
        groups += [up, down]
        up, down = shift(up, "z", 1), shift(down, "z", -1)
        go_up, go_down = shift(go_up, "z", 1), shift(go_down, "z", -1)
        groups += [up, down]
        up, down = shift(up[:64], "z", 1), shift(down[64:], "z", -1)
        go_up = jnp.concatenate([spread[640:704] + go_up, spread[704:768]])
        go_down = jnp.concatenate([spread[768:832], spread[832:896] + go_down])
        groups += [up, down]
        go_up, go_down, *groups = barrier(go_up, go_down, *groups)
        go_up, go_down = shift(go_up, "z", 1), shift(go_down, "z", -1)
        summed, tail = direct_products((pair, *held), groups, split, sum_at, from_at, place)

        tail = tail + swap(tail, "c", 1)
        go_up, go_down, tail = barrier(go_up, go_down, tail)
        go_up, go_down = spread[384:512] + go_up, spread[512:640] + go_down
        go_up, go_down, tail = barrier(go_up, go_down, tail)
        go_up, go_down = shift(go_up, "z", 1), shift(go_down, "z", -1)
        tail = tail + swap(tail, "x", 1)
        tail = tail + swap(tail, "x", 2)
        four = summed[:128] + swap(summed[128:], "x", 2)
        go_up, go_down, tail, four = barrier(go_up, go_down, tail, four)
        go_up, go_down = spread[128:256] + go_up, spread[256:384] + go_down
        go_up, go_down, tail = barrier(go_up, go_down, tail)
        energy = tail[:, 256:384]
        go_up, go_down = shift(go_up, "z", 1), shift(go_down, "z", -1)
        energy = energy + swap(energy, "y", 1)
        energy = energy + swap(energy, "y", 2)
        two = four[:64] + swap(four[64:], "x", 1)
        go_up, go_down, energy, two = barrier(go_up, go_down, energy, two)
        near, up, down, far = jnp.split(spread[0:128] + (go_up + go_down), 4)
        near, up, down, far, energy = barrier(near, up, down, far, energy)
        up, down, far = shift(up, "y", 1), shift(down, "y", -1), shift(far, "y", 2)
        column_part = two[:32] + swap(two[32:], "c", 1)
        energy = energy + swap(energy, "z", 1)
        energy = energy + swap(energy, "z", 2)
        if iteration > 0:
            cross, direction, images = call(
                mix_kernel, [SMALL, rows_of(32), rows_of(32)],
                tail, gram, curvature, images, direction, residual,
            )
        core = (tail, energy, swap(energy, "z", 4), near, up, down, far, column_part, residual)
        outs = [rows_of(32), rows_of(32), rows_of(32), rows_of(40), SMALL, SMALL]
        if iteration == 0:
            direction = residual
            solution, residual, images, message, gram, curvature = call(
                step_first_kernel, outs, *core
            )
        else:
            solution, residual, images, message, gram, curvature = call(
                step_kernel, outs, *core, cross, direction, images, solution
            )
    return (solution, residual)


def solution(mesh):
    fine = Mesh(mesh.devices.reshape(8, 4, 4, 2), AXES)
    return jax.shard_map(
        local,
        mesh=fine,
        in_specs=(P(None, AXES), P(AXES, None, None), P(AXES), P(AXES)),
        out_specs=(P(None, AXES), P(None, AXES)),
        check_vma=False,
    )
```
